1024 devices in a mesh: dp: 128 (over x, y_lo, z), group: 8 (over y_hi, core).
Axes of the slice: x: 4, y: 8 (y_hi: 4, y_lo: 2; y = y_hi * 2 + y_lo), z: 16, core: 2. Of those that a mesh axis runs over, the one named last changes fastest.
Arguments:
- activations: bfloat16 [65536, 2048], P('dp', 'group'), may hold values from -6 to 6
- cotangent: bfloat16 [65536, 704], P('dp'), may hold values from -0.0234375 to 0.0234375
- momentum: float32 [8, 256, 704], P('group', 'dp'), may hold values from -256 to 256, as said below
Outputs:
- update: bfloat16 [8, 256, 704], P('group', 'dp')
- momentum_new: float32 [8, 256, 704], P('group', 'dp')
The draws below stay inside these ranges and needn't reach their ends.
Inputs may be any that keep to these rules, and one draw needn't show every extreme that they name: The momentum buffer's entries.
All inputs are finite; a program needn't handle non-finite values.
Results may differ from the reference program's by a relative error of at most 0.015.
Values may be sent and summed in bfloat16 or wider, within the bound.
No kernel may reach another device: no remote copies, remote signals or barrier semaphores. Data moves between devices by JAX's collectives and lax.ppermute only.
A program may use at most 32 MiB of HBM per device.

```python
import jax
import jax.numpy as jnp

DM = 2048
FE = 704
ITERS = 3
TOKENS = 65536
GROUPS = 8
SLICE = 256


def draw_momentum(key, part):
    key = jax.random.fold_in(key, 7)
    key_base, key_rough = jax.random.split(key)
    shape = (GROUPS, SLICE, FE)
    position = (jnp.arange(SLICE, dtype=jnp.float32) / SLICE).reshape(1, SLICE, 1)
    base = jnp.clip(jax.random.normal(key_base, shape, jnp.float32), -6.0, 6.0)
    ramp = jnp.power(10.0, position)
    rough = jnp.exp(jax.random.uniform(key_rough, shape, jnp.float32, -0.35, 0.35))
    return (base * ramp * rough).astype(jnp.float32)


def block_scale(own_key, shape, cuts, smallest, largest):
    factor_of, own = 1.0, jax.random.fold_in(own_key, 6)
    for dim, shards_of in cuts:
        draws = jnp.exp(jax.random.uniform(jax.random.fold_in(own, dim), (shards_of,), jnp.float32, smallest / len(cuts), largest / len(cuts)))
        factor_of = factor_of * jnp.repeat(draws, shape[dim] // shards_of).reshape([-1 if axis == dim else 1 for axis in range(len(shape))])
    return factor_of


def centred(rng, extent, spread, limit, pieces=(), kind=jnp.bfloat16):
    entries = jax.random.normal(rng, extent, jnp.float32) * spread
    if len(pieces) > 0:
        entries = block_scale(rng, extent, pieces, -0.22, 0.18) * entries
    return jnp.clip(entries, min=-limit, max=limit).astype(kind)


def setup_inputs(seed: int = 0) -> dict:
    key_list = jax.random.split(jax.random.key(seed), 4)
    activations = centred(key_list[0], (TOKENS, DM), 1.0, 6.0, ((0, 128), (1, 8)))
    cotangent = centred(key_list[1], (TOKENS, FE), TOKENS ** -0.5, 0.0234375, ((0, 128),))
    momentum = draw_momentum(jax.random.fold_in(key_list[3], 71), 0)
    return dict(activations=activations, cotangent=cotangent, momentum=momentum)


quintic_a = 3.4445
quintic_b = -4.775
quintic_c = 2.0315

def reference(activations, cotangent, momentum):
    gradient = jnp.dot(activations.T, cotangent, preferred_element_type=jnp.float32)
    gradient = gradient.reshape(GROUPS, SLICE, FE)
    momentum_new = 0.95 * momentum + gradient
    direction = gradient + 0.95 * momentum_new
    frob = jnp.sqrt(jnp.sum(direction * direction))
    orthogonal = (direction / (frob + 1e-07)).astype(jnp.bfloat16).reshape(GROUPS * SLICE, FE)
    for sweep in range(ITERS):
        gram_matrix = jnp.dot(orthogonal.T, orthogonal, preferred_element_type=jnp.float32).astype(jnp.bfloat16)
        square = jnp.dot(gram_matrix, gram_matrix, preferred_element_type=jnp.float32)
        polynomial = (quintic_b * gram_matrix.astype(jnp.float32) + quintic_c * square).astype(jnp.bfloat16)
        product = jnp.dot(orthogonal, polynomial, preferred_element_type=jnp.float32)
        orthogonal = (quintic_a * orthogonal.astype(jnp.float32) + product).astype(jnp.bfloat16)
    step_scale = 0.2 * max(DM, FE) ** 0.5
    update = (step_scale * orthogonal.astype(jnp.float32)).astype(jnp.bfloat16)
    return (update.reshape(GROUPS, SLICE, FE), momentum_new)
```

```python
import jax
import jax.numpy as jnp
from jax import lax
from jax.experimental import pallas as pl
from jax.experimental.pallas import tpu as pltpu
from jax.sharding import Mesh, PartitionSpec as P

DM = 2048
FE = 704
ITERS = 3
WIDE = 768

quintic_a = 3.4445
quintic_b = -4.775
quintic_c = 2.0315

AXES = ("x", "ylo", "z", "yhi", "core")
SIZES = (4, 2, 16, 4, 2)
NEAR = ("x", "ylo")
FAR = ("z", "yhi")

f32 = jnp.float32
bf16 = jnp.bfloat16


def mm(a, b):
    return jnp.dot(a, b, preferred_element_type=f32)


def newton_schulz_kernel(mine_ref, other_ref, rows_ref, out_ref, gram_ref, poly_ref, left_ref, next_ref):
    total = jnp.zeros((128, 128), f32)
    for t in range(WIDE // 128):
        block = pl.ds(t * 128, 128)
        total += mine_ref[block, block] + other_ref[block, block].astype(f32)
    eye = lax.broadcasted_iota(jnp.int32, (128, 128), 0) == lax.broadcasted_iota(
        jnp.int32, (128, 128), 1
    )
    square_sum = jnp.sum(jnp.where(eye, total, 0.0), keepdims=True)
    scale = 1.0 / (jnp.sqrt(square_sum) + 1e-07)
    gram_ref[...] = ((mine_ref[...] + other_ref[...].astype(f32)) * scale * scale).astype(bf16)
    x = (rows_ref[...] * scale).astype(bf16)

    def right(rows, matrix_ref):
        return mm(rows, matrix_ref[...])

    def polynomial(g_ref):
        square = mm(g_ref[...], g_ref[...])
        poly_ref[...] = (quintic_b * g_ref[...].astype(f32) + quintic_c * square).astype(bf16)

    def step(rows):
        return (quintic_a * rows.astype(f32) + right(rows, poly_ref)).astype(bf16)

    polynomial(gram_ref)
    x = step(x)
    left_ref[...] = (
        quintic_a * gram_ref[...].astype(f32) + mm(poly_ref[...], gram_ref[...])
    ).astype(bf16)
    next_ref[...] = (
        quintic_a * left_ref[...].astype(f32) + mm(left_ref[...], poly_ref[...])
    ).astype(bf16)
    polynomial(next_ref)
    x = step(x)
    left_ref[...] = (
        quintic_a * next_ref[...].astype(f32) + mm(poly_ref[...], next_ref[...])
    ).astype(bf16)
    gram_ref[...] = (
        quintic_a * left_ref[...].astype(f32) + mm(left_ref[...], poly_ref[...])
    ).astype(bf16)
    once = right(x, gram_ref)
    twice = right(once.astype(bf16), gram_ref)
    x = (quintic_a * x.astype(f32) + (quintic_b * once + quintic_c * twice)).astype(bf16)
    step_scale = 0.2 * max(DM, FE) ** 0.5
    out_ref[...] = (step_scale * x.astype(f32)).astype(bf16)


def newton_schulz(mine, other, rows):
    return pl.pallas_call(
        newton_schulz_kernel,
        out_shape=jax.ShapeDtypeStruct((16, WIDE), bf16),
        in_specs=[pl.BlockSpec(memory_space=pltpu.VMEM)] * 3,
        out_specs=pl.BlockSpec(memory_space=pltpu.VMEM),
        scratch_shapes=[pltpu.VMEM((WIDE, WIDE), bf16)] * 4,
        compiler_params=pltpu.CompilerParams(vmem_limit_bytes=48 * 1024 * 1024),
    )(mine, other, rows)


def spread(block, axes, members):
    copies = jnp.broadcast_to(block[None], (members,) + block.shape)
    return lax.all_to_all(copies, axes, 0, 0, tiled=True)


def per_device(activations, cotangent, momentum):
    partial = lax.dot_general(
        activations, cotangent, (((0,), (0,)), ((), ())), preferred_element_type=f32
    ).astype(bf16)
    near = lax.all_to_all(partial.reshape(8, 32, FE), NEAR, 0, 0, tiled=True)
    near = jnp.sum(near.astype(f32), axis=0).astype(bf16)
    far = lax.all_to_all(near.reshape(16, 2, FE), "z", 0, 0, tiled=True)
    gradient = jnp.sum(far.astype(f32), axis=0)
    momentum_new = 0.95 * momentum[0] + gradient
    direction = gradient + 0.95 * momentum_new
    wide = jnp.pad(direction, ((0, 0), (0, WIDE - FE)))
    rows = spread(wide.astype(bf16), FAR, 64).reshape(128, WIDE)
    rows = spread(rows, NEAR, 8).reshape(1024, WIDE)
    mine = lax.dot_general(rows, rows, (((0,), (0,)), ((), ())), preferred_element_type=f32)
    other = lax.ppermute(mine.astype(bf16), "core", [(0, 1), (1, 0)])
    update = newton_schulz(mine, other, jnp.pad(wide, ((0, 14), (0, 0))))
    return (update[None, :2, :FE], momentum_new[None])


def solution(mesh):
    fine = Mesh(mesh.devices.reshape(SIZES), AXES)
    tokens, owners = ("x", "ylo", "z"), ("yhi", "core")
    in_specs = (P(tokens, owners), P(tokens, None), P(owners, tokens, None))
    out_specs = (P(owners, tokens, None), P(owners, tokens, None))
    return jax.shard_map(
        per_device, mesh=fine, in_specs=in_specs, out_specs=out_specs, check_vma=False
    )
```

```python
import jax
import jax.numpy as jnp
from jax import lax
from jax.experimental import pallas as pl
from jax.experimental.pallas import tpu as pltpu
from jax.sharding import Mesh, PartitionSpec as P

DM = 2048
FE = 704
ITERS = 3
WIDE = 768
SHARE = 256
TILE = 256
BLOCK = 16

quintic_a = 3.4445
quintic_b = -4.775
quintic_c = 2.0315
step_scale = 0.2 * max(DM, FE) ** 0.5

AXES = ("x", "ylo", "zhi", "zlo", "yhi", "core")
SIZES = (4, 2, 8, 2, 4, 2)
NEAR = ("x", "ylo", "zlo")
FAR = "zhi"
OWNERS = "yhi"

f32 = jnp.float32
bf16 = jnp.bfloat16


def mm(a, b):
    return jnp.dot(a, b, preferred_element_type=f32)


def mm_nt(a, b):
    return lax.dot_general(a, b, (((1,), (1,)), ((), ())), preferred_element_type=f32)


def kernel_call(kernel, out_shape, n_in, scratch=(), mib=32):
    return pl.pallas_call(
        kernel,
        out_shape=out_shape,
        in_specs=[pl.BlockSpec(memory_space=pltpu.VMEM)] * n_in,
        out_specs=jax.tree.map(lambda _: pl.BlockSpec(memory_space=pltpu.VMEM), out_shape),
        scratch_shapes=list(scratch),
        compiler_params=pltpu.CompilerParams(vmem_limit_bytes=mib * 1024 * 1024),
    )


def gradient_kernel(act_ref, cot_ref, out_ref):
    to = lax.broadcasted_iota(jnp.int32, (SHARE, SHARE), 0)
    source = lax.broadcasted_iota(jnp.int32, (SHARE, SHARE), 1)
    wanted = (to & ~31) + ((to & 15) >> 1) * 4 + ((to & 31) >> 4) * 2 + (to & 1)
    order = jnp.where(wanted == source, 1.0, 0.0).astype(bf16)
    left = mm_nt(order, act_ref[...]).astype(bf16)
    out_ref[:, :FE] = mm_nt(left, cot_ref[...]).astype(bf16)
    out_ref[:, FE:] = jnp.zeros((SHARE, WIDE - FE), bf16)


def own_rows_mask():
    row = lax.broadcasted_iota(jnp.int32, (BLOCK, WIDE), 0)
    return (row >> 1) == lax.axis_index(FAR)


def place_rows(mom_ref):
    row = lax.broadcasted_iota(jnp.int32, (BLOCK, FE), 0)
    first = jnp.broadcast_to(mom_ref[0:1, :], (BLOCK, FE))
    second = jnp.broadcast_to(mom_ref[1:2, :], (BLOCK, FE))
    rows = jnp.where((row & 1) == 0, first, second)
    return jnp.concatenate([rows, jnp.zeros((BLOCK, WIDE - FE), f32)], axis=1)


def share_kernel(near_ref, mom_ref, exact_ref, out_ref):
    partial = jnp.sum(near_ref[...].astype(f32), axis=0)
    own = jnp.where(own_rows_mask(), place_rows(mom_ref), 0.0)
    share = 1.95 * partial + (0.95 * 0.95) * own
    exact_ref[...] = share
    out_ref[...] = jnp.broadcast_to(share.astype(bf16)[None], out_ref.shape)


def direction_kernel(far_ref, exact_ref, mom_ref, rows_ref, own_ref, new_ref):
    total = jnp.sum(far_ref[...].astype(f32), axis=0)
    rows_ref[...] = jnp.broadcast_to(total.astype(bf16)[None], rows_ref.shape)
    exact = exact_ref[...]
    better = total + (exact - exact.astype(bf16).astype(f32))
    mine = jnp.where(own_rows_mask(), better, 0.0)
    odd = (lax.broadcasted_iota(jnp.int32, (BLOCK, WIDE), 0) & 1) == 1
    first = jnp.sum(jnp.where(odd, 0.0, mine), axis=0, keepdims=True)
    second = jnp.sum(jnp.where(odd, mine, 0.0), axis=0, keepdims=True)
    own_ref[...] = jnp.zeros_like(own_ref)
    own_ref[0:1, :] = first
    own_ref[1:2, :] = second
    for r, direction in enumerate((first, second)):
        old = mom_ref[r : r + 1, :]
        gradient = (direction[:, :FE] - (0.95 * 0.95) * old) / 1.95
        new_ref[r : r + 1, :] = 0.95 * old + gradient


def newton_schulz_kernel(
    mine_ref, other_ref, rows_ref, out_ref, gram_ref, poly_ref, left_ref, next_ref
):
    total = jnp.zeros((128, 128), f32)
    for t in range(WIDE // 128):
        block = pl.ds(t * 128, 128)
        total += mine_ref[block, block] + other_ref[block, block].astype(f32)
    eye = lax.broadcasted_iota(jnp.int32, (128, 128), 0) == lax.broadcasted_iota(
        jnp.int32, (128, 128), 1
    )
    square_sum = jnp.sum(jnp.where(eye, total, 0.0), keepdims=True)
    scale = 1.0 / (jnp.sqrt(square_sum) + 1e-07)
    gram_ref[...] = ((mine_ref[...] + other_ref[...].astype(f32)) * scale * scale).astype(bf16)
    x = (rows_ref[...] * scale).astype(bf16)

    def symmetric(to_ref, a_ref, b_ref, finish):
        for i in range(WIDE // TILE):
            rows, cols = pl.ds(i * TILE, TILE), pl.ds(i * TILE, WIDE - i * TILE)
            value = finish(rows, cols, mm(a_ref[rows, :], b_ref[:, cols])).astype(bf16)
            to_ref[rows, cols] = value
            for j in range(i + 1, WIDE // TILE):
                at = (j - i) * TILE
                to_ref[pl.ds(j * TILE, TILE), rows] = value[:, at : at + TILE].T

    def polynomial(g_ref):
        def finish(rows, cols, square):
            return quintic_b * g_ref[rows, cols].astype(f32) + quintic_c * square

        symmetric(poly_ref, g_ref, g_ref, finish)

    def one_side(to_ref, a_ref, b_ref, base_ref):
        def finish(rows, cols, product):
            return quintic_a * base_ref[rows, cols].astype(f32) + product

        symmetric(to_ref, a_ref, b_ref, finish)

    def step(rows):
        return quintic_a * rows.astype(f32) + mm(rows, poly_ref[...])

    polynomial(gram_ref)
    x = step(x).astype(bf16)
    one_side(left_ref, poly_ref, gram_ref, gram_ref)
    one_side(next_ref, left_ref, poly_ref, left_ref)
    polynomial(next_ref)
    x = step(x).astype(bf16)

    def last_gram(rows):
        rows = step(rows).astype(bf16)
        return step(mm(rows, next_ref[...]).astype(bf16))

    once = last_gram(x)
    twice = last_gram(once.astype(bf16))
    x = (quintic_a * x.astype(f32) + (quintic_b * once + quintic_c * twice)).astype(bf16)
    out_ref[...] = (step_scale * x.astype(f32)).astype(bf16)[:2, :FE]


def shape(dims, dtype):
    return jax.ShapeDtypeStruct(dims, dtype)


def exchange(blocks, axes):
    return lax.all_to_all(blocks, axes, 0, 0, tiled=True)


def per_device(activations, cotangent, momentum):
    momentum = momentum[0]
    partial = kernel_call(gradient_kernel, shape((SHARE, WIDE), bf16), 2)(activations, cotangent.T)
    near = exchange(partial.reshape(16, BLOCK, WIDE), NEAR)
    exact, share = kernel_call(
        share_kernel, (shape((BLOCK, WIDE), f32), shape((8, BLOCK, WIDE), bf16)), 2
    )(near, momentum)
    far = exchange(share, FAR)
    rows, own, momentum_new = kernel_call(
        direction_kernel,
        (shape((4, BLOCK, WIDE), bf16), shape((16, WIDE), f32), shape((2, FE), f32)),
        3,
    )(far, exact, momentum)
    rows = exchange(rows, OWNERS).reshape(64, WIDE)
    rows = exchange(jnp.broadcast_to(rows[None], (16, 64, WIDE)), NEAR).reshape(1024, WIDE)
    mine = lax.dot_general(rows, rows, (((0,), (0,)), ((), ())), preferred_element_type=f32)
    other = lax.ppermute(mine.astype(bf16), "core", [(0, 1), (1, 0)])
    update = kernel_call(
        newton_schulz_kernel, shape((2, FE), bf16), 3, [pltpu.VMEM((WIDE, WIDE), bf16)] * 4, 48
    )(mine, other, own)
    return (update[None], momentum_new[None])


def solution(mesh):
    fine = Mesh(mesh.devices.reshape(SIZES), AXES)
    tokens, owners = ("x", "ylo", "zhi", "zlo"), ("yhi", "core")
    in_specs = (P(tokens, owners), P(tokens, None), P(owners, tokens, None))
    out_specs = (P(owners, tokens, None), P(owners, tokens, None))
    return jax.shard_map(
        per_device, mesh=fine, in_specs=in_specs, out_specs=out_specs, check_vma=False
    )
```

```python
import jax
import jax.numpy as jnp
from jax import lax
from jax.experimental import pallas as pl
from jax.experimental.pallas import tpu as pltpu
from jax.sharding import Mesh, PartitionSpec as P

DM = 2048
FE = 704
ITERS = 3
WIDE = 768
SHARE = 256
TILE = 256
BLOCK = 16

quintic_a = 3.4445
quintic_b = -4.775
quintic_c = 2.0315
step_scale = 0.2 * max(DM, FE) ** 0.5

AXES = ("x", "ylo", "zhi", "zlo", "yhi", "core")
SIZES = (4, 2, 8, 2, 4, 2)
NEAR = ("x", "ylo", "zlo")
FAR = "zhi"
OWNERS = "yhi"

f32 = jnp.float32
bf16 = jnp.bfloat16


def mm(a, b):
    return jnp.dot(a, b, preferred_element_type=f32)


def mm_nt(a, b):
    return lax.dot_general(a, b, (((1,), (1,)), ((), ())), preferred_element_type=f32)


def kernel_call(kernel, out_shape, n_in, scratch=(), mib=32, space=pltpu.VMEM):
    return pl.pallas_call(
        kernel,
        out_shape=out_shape,
        in_specs=[pl.BlockSpec(memory_space=space)] * n_in,
        out_specs=jax.tree.map(lambda _: pl.BlockSpec(memory_space=pltpu.VMEM), out_shape),
        scratch_shapes=list(scratch),
        compiler_params=pltpu.CompilerParams(vmem_limit_bytes=mib * 1024 * 1024),
    )


def gradient_kernel(act_hbm, cot_hbm, out_ref, act_ref, cot_ref, act_sem, cot_sems):
    fetch_act = pltpu.make_async_copy(act_hbm, act_ref, act_sem)
    fetch_act.start()
    fetches = []
    for j, at in enumerate(range(0, FE, TILE)):
        part = pl.ds(at, min(TILE, FE - at))
        fetches.append(
            (part, pltpu.make_async_copy(cot_hbm.at[part], cot_ref.at[part], cot_sems.at[j]))
        )
        fetches[-1][1].start()
    to = lax.broadcasted_iota(jnp.int32, (SHARE, SHARE), 0)
    source = lax.broadcasted_iota(jnp.int32, (SHARE, SHARE), 1)
    wanted = (to & ~31) + ((to & 15) >> 1) * 4 + ((to & 31) >> 4) * 2 + (to & 1)
    order = jnp.where(wanted == source, 1.0, 0.0).astype(bf16)
    out_ref[:, FE:] = jnp.zeros((SHARE, WIDE - FE), bf16)
    fetch_act.wait()
    left = mm_nt(order, act_ref[...]).astype(bf16)
    for part, fetch in fetches:
        fetch.wait()
        out_ref[:, part] = mm_nt(left, cot_ref[part, :]).astype(bf16)


def own_rows_mask():
    row = lax.broadcasted_iota(jnp.int32, (BLOCK, WIDE), 0)
    return (row >> 1) == lax.axis_index(FAR)


def place_rows(mom_ref):
    row = lax.broadcasted_iota(jnp.int32, (BLOCK, FE), 0)
    first = jnp.broadcast_to(mom_ref[0:1, :], (BLOCK, FE))
    second = jnp.broadcast_to(mom_ref[1:2, :], (BLOCK, FE))
    rows = jnp.where((row & 1) == 0, first, second)
    return jnp.concatenate([rows, jnp.zeros((BLOCK, WIDE - FE), f32)], axis=1)


def share_kernel(near_ref, mom_ref, exact_ref, out_ref):
    partial = jnp.sum(near_ref[...].astype(f32), axis=0)
    own = jnp.where(own_rows_mask(), place_rows(mom_ref), 0.0)
    share = 1.95 * partial + (0.95 * 0.95) * own
    exact_ref[...] = share
    out_ref[...] = jnp.broadcast_to(share.astype(bf16)[None], out_ref.shape)


def direction_kernel(far_ref, exact_ref, rows_ref, own_ref):
    total = jnp.sum(far_ref[...].astype(f32), axis=0)
    rows_ref[...] = jnp.broadcast_to(total.astype(bf16)[None], rows_ref.shape)
    exact = exact_ref[...]
    better = total + (exact - exact.astype(bf16).astype(f32))
    mine = jnp.where(own_rows_mask(), better, 0.0)
    odd = (lax.broadcasted_iota(jnp.int32, (BLOCK, WIDE), 0) & 1) == 1
    own_ref[...] = jnp.zeros_like(own_ref)
    own_ref[0:1, :] = jnp.sum(jnp.where(odd, 0.0, mine), axis=0, keepdims=True)
    own_ref[1:2, :] = jnp.sum(jnp.where(odd, mine, 0.0), axis=0, keepdims=True)


def packed_blocks():
    at = 0
    for first in range(0, WIDE, TILE):
        yield first, at, WIDE - first
        at += WIDE - first


def gram_kernel(rows_ref, out_ref):
    for first, at, width in packed_blocks():
        out_ref[:, at : at + width] = lax.dot_general(
            rows_ref[:, first : first + TILE],
            rows_ref[:, first:],
            (((0,), (0,)), ((), ())),
            preferred_element_type=f32,
        ).astype(bf16)


def newton_schulz_kernel(
    mine_ref, other_ref, rows_ref, out_ref, gram_ref, poly_ref, left_ref, next_ref
):
    total = jnp.zeros((128, 128), f32)
    for _, at, _ in packed_blocks():
        for half in range(0, TILE, 128):
            rows, cols = pl.ds(half, 128), pl.ds(at + half, 128)
            total += mine_ref[rows, cols].astype(f32) + other_ref[rows, cols].astype(f32)
    eye = lax.broadcasted_iota(jnp.int32, (128, 128), 0) == lax.broadcasted_iota(
        jnp.int32, (128, 128), 1
    )
    square_sum = jnp.sum(jnp.where(eye, total, 0.0), keepdims=True)
    scale = 1.0 / (jnp.sqrt(square_sum) + 1e-07)
    x = (rows_ref[...] * scale).astype(bf16)

    def store_symmetric(to_ref, first, value):
        rows = pl.ds(first, TILE)
        to_ref[rows, pl.ds(first, WIDE - first)] = value
        for later in range(first + TILE, WIDE, TILE):
            at = later - first
            to_ref[pl.ds(later, TILE), rows] = value[:, at : at + TILE].T

    for first, at, width in packed_blocks():
        cols = pl.ds(at, width)
        both = mine_ref[:, cols].astype(f32) + other_ref[:, cols].astype(f32)
        store_symmetric(gram_ref, first, (both * scale * scale).astype(bf16))

    def symmetric(to_ref, a_ref, b_ref, finish):
        for first in range(0, WIDE, TILE):
            rows, cols = pl.ds(first, TILE), pl.ds(first, WIDE - first)
            value = finish(rows, cols, mm(a_ref[rows, :], b_ref[:, cols])).astype(bf16)
            store_symmetric(to_ref, first, value)

    def polynomial(g_ref):
        def finish(rows, cols, square):
            return quintic_b * g_ref[rows, cols].astype(f32) + quintic_c * square

        symmetric(poly_ref, g_ref, g_ref, finish)

    def one_side(to_ref, a_ref, b_ref, base_ref):
        def finish(rows, cols, product):
            return quintic_a * base_ref[rows, cols].astype(f32) + product

        symmetric(to_ref, a_ref, b_ref, finish)

    def step(rows):
        return quintic_a * rows.astype(f32) + mm(rows, poly_ref[...])

    polynomial(gram_ref)
    x = step(x).astype(bf16)
    one_side(left_ref, poly_ref, gram_ref, gram_ref)
    one_side(next_ref, left_ref, poly_ref, left_ref)
    polynomial(next_ref)
    x = step(x).astype(bf16)

    def last_gram(rows):
        rows = step(rows).astype(bf16)
        return step(mm(rows, next_ref[...]).astype(bf16))

    once = last_gram(x)
    twice = last_gram(once.astype(bf16))
    x = (quintic_a * x.astype(f32) + (quintic_b * once + quintic_c * twice)).astype(bf16)
    out_ref[...] = (step_scale * x.astype(f32)).astype(bf16)[:2, :FE]


def shape(dims, dtype):
    return jax.ShapeDtypeStruct(dims, dtype)


def exchange(blocks, axes):
    return lax.all_to_all(blocks, axes, 0, 0, tiled=True)


def per_device(activations, cotangent, momentum):
    momentum = momentum[0]
    partial = kernel_call(
        gradient_kernel,
        shape((SHARE, WIDE), bf16),
        2,
        [
            pltpu.VMEM((512, SHARE), bf16),
            pltpu.VMEM((FE, 512), bf16),
            pltpu.SemaphoreType.DMA,
            pltpu.SemaphoreType.DMA((3,)),
        ],
        mib=60,
        space=pltpu.HBM,
    )(activations, cotangent.T)
    near = exchange(partial.reshape(16, BLOCK, WIDE), NEAR)
    exact, share = kernel_call(
        share_kernel, (shape((BLOCK, WIDE), f32), shape((8, BLOCK, WIDE), bf16)), 2
    )(near, momentum)
    far = exchange(share, FAR)
    rows, own = kernel_call(
        direction_kernel, (shape((4, BLOCK, WIDE), bf16), shape((16, WIDE), f32)), 2
    )(far, exact)
    rows = exchange(rows, OWNERS).reshape(64, WIDE)
    rows = exchange(jnp.broadcast_to(rows[None], (16, 64, WIDE)), NEAR).reshape(1024, WIDE)
    mine = kernel_call(gram_kernel, shape((TILE, 1536), bf16), 1)(rows)
    other = lax.ppermute(mine, "core", [(0, 1), (1, 0)])
    gradient = (own[:2, :FE] - (0.95 * 0.95) * momentum) / 1.95
    momentum_new = 0.95 * momentum + gradient
    update = kernel_call(
        newton_schulz_kernel, shape((2, FE), bf16), 3, [pltpu.VMEM((WIDE, WIDE), bf16)] * 4, mib=48
    )(mine, other, own)
    return (update[None], momentum_new[None])


def solution(mesh):
    fine = Mesh(mesh.devices.reshape(SIZES), AXES)
    tokens, owners = ("x", "ylo", "zhi", "zlo"), ("yhi", "core")
    in_specs = (P(tokens, owners), P(tokens, None), P(owners, tokens, None))
    out_specs = (P(owners, tokens, None), P(owners, tokens, None))
    return jax.shard_map(
        per_device, mesh=fine, in_specs=in_specs, out_specs=out_specs, check_vma=False
    )
```

```python
import jax
import jax.numpy as jnp
from jax import lax
from jax.experimental import pallas as pl
from jax.experimental.pallas import tpu as pltpu
from jax.sharding import Mesh, PartitionSpec as P

DM = 2048
FE = 704
ITERS = 3
WIDE = 768
SHARE = 256
TILE = 256
BLOCK = 16

quintic_a = 3.4445
quintic_b = -4.775
quintic_c = 2.0315
step_scale = 0.2 * max(DM, FE) ** 0.5

AXES = ("x", "ylo", "zhi", "zlo", "yhi", "core")
SIZES = (4, 2, 8, 2, 4, 2)
NEAR = ("x", "ylo", "zlo")
FAR = "zhi"
OWNERS = "yhi"

f32 = jnp.float32
bf16 = jnp.bfloat16


def mm(a, b):
    return jnp.dot(a, b, preferred_element_type=f32)


def mm_nt(a, b):
    return lax.dot_general(a, b, (((1,), (1,)), ((), ())), preferred_element_type=f32)


def kernel_call(kernel, out_shape, n_in, scratch=(), mib=32):
    return pl.pallas_call(
        kernel,
        out_shape=out_shape,
        in_specs=[pl.BlockSpec(memory_space=pltpu.VMEM)] * n_in,
        out_specs=jax.tree.map(lambda _: pl.BlockSpec(memory_space=pltpu.VMEM), out_shape),
        scratch_shapes=list(scratch),
        compiler_params=pltpu.CompilerParams(vmem_limit_bytes=mib * 1024 * 1024),
    )


def gradient_kernel(act_ref, cot_ref, out_ref):
    to = lax.broadcasted_iota(jnp.int32, (SHARE, SHARE), 0)
    source = lax.broadcasted_iota(jnp.int32, (SHARE, SHARE), 1)
    wanted = (to & ~31) + ((to & 15) >> 1) * 4 + ((to & 31) >> 4) * 2 + (to & 1)
    order = jnp.where(wanted == source, 1.0, 0.0).astype(bf16)
    left = mm_nt(order, act_ref[...]).astype(bf16)
    out_ref[:, :FE] = mm_nt(left, cot_ref[...]).astype(bf16)
    out_ref[:, FE:] = jnp.zeros((SHARE, WIDE - FE), bf16)


def own_rows_mask():
    row = lax.broadcasted_iota(jnp.int32, (BLOCK, WIDE), 0)
    return (row >> 1) == lax.axis_index(FAR)


def place_rows(mom_ref):
    row = lax.broadcasted_iota(jnp.int32, (BLOCK, FE), 0)
    first = jnp.broadcast_to(mom_ref[0:1, :], (BLOCK, FE))
    second = jnp.broadcast_to(mom_ref[1:2, :], (BLOCK, FE))
    rows = jnp.where((row & 1) == 0, first, second)
    return jnp.concatenate([rows, jnp.zeros((BLOCK, WIDE - FE), f32)], axis=1)


def share_kernel(near_ref, mom_ref, exact_ref, out_ref):
    partial = jnp.sum(near_ref[...].astype(f32), axis=0)
    own = jnp.where(own_rows_mask(), place_rows(mom_ref), 0.0)
    share = 1.95 * partial + (0.95 * 0.95) * own
    exact_ref[...] = share
    out_ref[...] = jnp.broadcast_to(share.astype(bf16)[None], out_ref.shape)


def direction_kernel(far_ref, exact_ref, rows_ref, own_ref):
    total = jnp.sum(far_ref[...].astype(f32), axis=0)
    rows_ref[...] = jnp.broadcast_to(total.astype(bf16)[None], rows_ref.shape)
    exact = exact_ref[...]
    better = total + (exact - exact.astype(bf16).astype(f32))
    mine = jnp.where(own_rows_mask(), better, 0.0)
    odd = (lax.broadcasted_iota(jnp.int32, (BLOCK, WIDE), 0) & 1) == 1
    own_ref[...] = jnp.zeros_like(own_ref)
    own_ref[0:1, :] = jnp.sum(jnp.where(odd, 0.0, mine), axis=0, keepdims=True)
    own_ref[1:2, :] = jnp.sum(jnp.where(odd, mine, 0.0), axis=0, keepdims=True)


def packed_blocks():
    at = 0
    for first in range(0, WIDE, TILE):
        yield first, at, WIDE - first
        at += WIDE - first


def gram_kernel(rows_ref, out_ref):
    for first, at, width in packed_blocks():
        out_ref[:, at : at + width] = lax.dot_general(
            rows_ref[:, first : first + TILE],
            rows_ref[:, first:],
            (((0,), (0,)), ((), ())),
            preferred_element_type=f32,
        ).astype(bf16)


def newton_schulz_kernel(
    mine_ref, other_ref, rows_ref, out_ref, gram_ref, poly_ref, left_ref, next_ref
):
    total = jnp.zeros((128, 128), f32)
    for _, at, _ in packed_blocks():
        for half in range(0, TILE, 128):
            rows, cols = pl.ds(half, 128), pl.ds(at + half, 128)
            total += mine_ref[rows, cols].astype(f32) + other_ref[rows, cols].astype(f32)
    eye = lax.broadcasted_iota(jnp.int32, (128, 128), 0) == lax.broadcasted_iota(
        jnp.int32, (128, 128), 1
    )
    square_sum = jnp.sum(jnp.where(eye, total, 0.0), keepdims=True)
    scale = 1.0 / (jnp.sqrt(square_sum) + 1e-07)
    x = (rows_ref[...] * scale).astype(bf16)

    def store_symmetric(to_ref, first, value):
        rows = pl.ds(first, TILE)
        to_ref[rows, pl.ds(first, WIDE - first)] = value
        for later in range(first + TILE, WIDE, TILE):
            at = later - first
            to_ref[pl.ds(later, TILE), rows] = value[:, at : at + TILE].T

    for first, at, width in packed_blocks():
        cols = pl.ds(at, width)
        both = mine_ref[:, cols].astype(f32) + other_ref[:, cols].astype(f32)
        store_symmetric(gram_ref, first, (both * scale * scale).astype(bf16))

    def symmetric(to_ref, a_ref, b_ref, finish):
        for first in range(0, WIDE, TILE):
            rows, cols = pl.ds(first, TILE), pl.ds(first, WIDE - first)
            value = finish(rows, cols, mm(a_ref[rows, :], b_ref[:, cols])).astype(bf16)
            store_symmetric(to_ref, first, value)

    def polynomial(g_ref):
        def finish(rows, cols, square):
            return quintic_b * g_ref[rows, cols].astype(f32) + quintic_c * square

        symmetric(poly_ref, g_ref, g_ref, finish)

    def one_side(to_ref, a_ref, b_ref, base_ref):
        def finish(rows, cols, product):
            return quintic_a * base_ref[rows, cols].astype(f32) + product

        symmetric(to_ref, a_ref, b_ref, finish)

    def step(rows):
        return quintic_a * rows.astype(f32) + mm(rows, poly_ref[...])

    polynomial(gram_ref)
    x = step(x).astype(bf16)
    one_side(left_ref, poly_ref, gram_ref, gram_ref)
    one_side(next_ref, left_ref, poly_ref, left_ref)
    polynomial(next_ref)
    x = step(x).astype(bf16)

    def last_gram(rows):
        rows = step(rows).astype(bf16)
        return step(mm(rows, next_ref[...]).astype(bf16))

    once = last_gram(x)
    twice = last_gram(once.astype(bf16))
    x = (quintic_a * x.astype(f32) + (quintic_b * once + quintic_c * twice)).astype(bf16)
    out_ref[...] = (step_scale * x.astype(f32)).astype(bf16)[:2, :FE]


def shape(dims, dtype):
    return jax.ShapeDtypeStruct(dims, dtype)


def exchange(blocks, axes):
    return lax.all_to_all(blocks, axes, 0, 0, tiled=True)


def per_device(activations, cotangent, momentum):
    momentum = momentum[0]
    partial = kernel_call(gradient_kernel, shape((SHARE, WIDE), bf16), 2)(activations, cotangent.T)
    near = exchange(partial.reshape(16, BLOCK, WIDE), NEAR)
    exact, share = kernel_call(
        share_kernel, (shape((BLOCK, WIDE), f32), shape((8, BLOCK, WIDE), bf16)), 2
    )(near, momentum)
    far = exchange(share, FAR)
    rows, own = kernel_call(
        direction_kernel, (shape((4, BLOCK, WIDE), bf16), shape((16, WIDE), f32)), 2
    )(far, exact)
    rows = exchange(rows, OWNERS).reshape(64, WIDE)
    rows = exchange(jnp.broadcast_to(rows[None], (16, 64, WIDE)), NEAR).reshape(1024, WIDE)
    mine = kernel_call(gram_kernel, shape((TILE, 1536), bf16), 1)(rows)
    other = lax.ppermute(mine, "core", [(0, 1), (1, 0)])
    gradient = (own[:2, :FE] - (0.95 * 0.95) * momentum) / 1.95
    momentum_new = 0.95 * momentum + gradient
    update = kernel_call(
        newton_schulz_kernel, shape((2, FE), bf16), 3, [pltpu.VMEM((WIDE, WIDE), bf16)] * 4, mib=48
    )(mine, other, own)
    return (update[None], momentum_new[None])


def solution(mesh):
    fine = Mesh(mesh.devices.reshape(SIZES), AXES)
    tokens, owners = ("x", "ylo", "zhi", "zlo"), ("yhi", "core")
    in_specs = (P(tokens, owners), P(tokens, None), P(owners, tokens, None))
    out_specs = (P(owners, tokens, None), P(owners, tokens, None))
    return jax.shard_map(
        per_device, mesh=fine, in_specs=in_specs, out_specs=out_specs, check_vma=False
    )
```

```python
import jax
import jax.numpy as jnp
from jax import lax
from jax.experimental import pallas as pl
from jax.experimental.pallas import tpu as pltpu
from jax.sharding import Mesh, PartitionSpec as P

DM = 2048
FE = 704
ITERS = 3
WIDE = 768
SHARE = 256
TILE = 256
BLOCK = 16

quintic_a = 3.4445
quintic_b = -4.775
quintic_c = 2.0315
step_scale = 0.2 * max(DM, FE) ** 0.5

AXES = ("x", "ylo", "zhi", "zlo", "yhi", "core")
SIZES = (4, 2, 8, 2, 4, 2)
NEAR = ("x", "ylo", "zlo")
FAR = "zhi"
OWNERS = "yhi"

f32 = jnp.float32
COST = pl.CostEstimate(flops=4_000_000_000, bytes_accessed=1_000_000, transcendentals=0)
bf16 = jnp.bfloat16


def mm(a, b):
    return jnp.dot(a, b, preferred_element_type=f32)


def mm_nt(a, b):
    return lax.dot_general(a, b, (((1,), (1,)), ((), ())), preferred_element_type=f32)


def kernel_call(kernel, out_shape, n_in, scratch=(), mib=32, cost=None):
    return pl.pallas_call(
        kernel,
        out_shape=out_shape,
        in_specs=[pl.BlockSpec(memory_space=pltpu.VMEM)] * n_in,
        out_specs=jax.tree.map(lambda _: pl.BlockSpec(memory_space=pltpu.VMEM), out_shape),
        scratch_shapes=list(scratch),
        cost_estimate=cost,
        compiler_params=pltpu.CompilerParams(vmem_limit_bytes=mib * 1024 * 1024),
    )


def order_kernel(act_ref, out_ref):
    to = lax.broadcasted_iota(jnp.int32, (SHARE, SHARE), 0)
    source = lax.broadcasted_iota(jnp.int32, (SHARE, SHARE), 1)
    wanted = (to & ~31) + ((to & 15) >> 1) * 4 + ((to & 31) >> 4) * 2 + (to & 1)
    order = jnp.where(wanted == source, 1.0, 0.0).astype(bf16)
    out_ref[...] = mm_nt(order, act_ref[...]).astype(bf16)


def gradient_kernel(left_ref, cot_ref, out_ref):
    out_ref[:, :FE] = mm_nt(left_ref[...], cot_ref[...]).astype(bf16)
    out_ref[:, FE:] = jnp.zeros((SHARE, WIDE - FE), bf16)


def own_rows_mask():
    row = lax.broadcasted_iota(jnp.int32, (BLOCK, WIDE), 0)
    return (row >> 1) == lax.axis_index(FAR)


def place_rows(mom_ref):
    row = lax.broadcasted_iota(jnp.int32, (BLOCK, FE), 0)
    first = jnp.broadcast_to(mom_ref[0:1, :], (BLOCK, FE))
    second = jnp.broadcast_to(mom_ref[1:2, :], (BLOCK, FE))
    rows = jnp.where((row & 1) == 0, first, second)
    return jnp.concatenate([rows, jnp.zeros((BLOCK, WIDE - FE), f32)], axis=1)


def share_kernel(near_ref, mom_ref, exact_ref, out_ref):
    partial = jnp.sum(near_ref[...].astype(f32), axis=0)
    own = jnp.where(own_rows_mask(), place_rows(mom_ref), 0.0)
    share = 1.95 * partial + (0.95 * 0.95) * own
    exact_ref[...] = share
    out_ref[...] = jnp.broadcast_to(share.astype(bf16)[None], out_ref.shape)


def direction_kernel(far_ref, exact_ref, rows_ref, own_ref):
    total = jnp.sum(far_ref[...].astype(f32), axis=0)
    rows_ref[...] = jnp.broadcast_to(total.astype(bf16)[None], rows_ref.shape)
    exact = exact_ref[...]
    better = total + (exact - exact.astype(bf16).astype(f32))
    mine = jnp.where(own_rows_mask(), better, 0.0)
    odd = (lax.broadcasted_iota(jnp.int32, (BLOCK, WIDE), 0) & 1) == 1
    own_ref[...] = jnp.zeros_like(own_ref)
    own_ref[0:1, :] = jnp.sum(jnp.where(odd, 0.0, mine), axis=0, keepdims=True)
    own_ref[1:2, :] = jnp.sum(jnp.where(odd, mine, 0.0), axis=0, keepdims=True)


def packed_blocks():
    at = 0
    for first in range(0, WIDE, TILE):
        yield first, at, WIDE - first
        at += WIDE - first


HALF = 32
ROWS = 64
PACKED = 352
TAIL = 640


def pack_kernel(rows_ref, out_ref):
    for at in range(0, TAIL, 128):
        tile = rows_ref[:, at : at + 128]
        out_ref[:, at // 2 : at // 2 + ROWS, :] = jnp.broadcast_to(tile[None], (16, ROWS, 128))
    upper = rows_ref[:HALF, TAIL:].astype(f32)
    lower = pltpu.roll(rows_ref[HALF:, TAIL:].astype(f32), 64, 1)
    lane = lax.broadcasted_iota(jnp.int32, (HALF, 128), 1)
    tile = jnp.where(lane < 64, upper, lower).astype(bf16)
    out_ref[:, TAIL // 2 :, :] = jnp.broadcast_to(tile[None], (16, HALF, 128))


def gram_kernel(packed_ref, out_ref, rows_ref):
    lane = lax.broadcasted_iota(jnp.int32, (HALF, 128), 1)
    for m in range(16):
        first = m * ROWS
        for at in range(0, TAIL, 128):
            rows_ref[first : first + ROWS, at : at + 128] = packed_ref[m, at // 2 : at // 2 + ROWS, :]
        tile = packed_ref[m, TAIL // 2 :, :].astype(f32)
        upper = jnp.where(lane < 64, tile, 0.0).astype(bf16)
        lower = jnp.where(lane < 64, pltpu.roll(tile, 64, 1), 0.0).astype(bf16)
        rows_ref[first : first + HALF, TAIL:] = upper
        rows_ref[first + HALF : first + ROWS, TAIL:] = lower
    for first, at, width in packed_blocks():
        out_ref[:, at : at + width] = lax.dot_general(
            rows_ref[:, first : first + TILE],
            rows_ref[:, first:],
            (((0,), (0,)), ((), ())),
            preferred_element_type=f32,
        ).astype(bf16)


def newton_schulz_kernel(
    mine_ref, other_ref, rows_ref, out_ref, gram_ref, poly_ref, left_ref, next_ref
):
    total = jnp.zeros((128, 128), f32)
    for _, at, _ in packed_blocks():
        for half in range(0, TILE, 128):
            rows, cols = pl.ds(half, 128), pl.ds(at + half, 128)
            total += mine_ref[rows, cols].astype(f32) + other_ref[rows, cols].astype(f32)
    eye = lax.broadcasted_iota(jnp.int32, (128, 128), 0) == lax.broadcasted_iota(
        jnp.int32, (128, 128), 1
    )
    square_sum = jnp.sum(jnp.where(eye, total, 0.0), keepdims=True)
    scale = 1.0 / (jnp.sqrt(square_sum) + 1e-07)
    x = (rows_ref[...] * scale).astype(bf16)

    def store_symmetric(to_ref, first, value):
        rows = pl.ds(first, TILE)
        to_ref[rows, pl.ds(first, WIDE - first)] = value
        for later in range(first + TILE, WIDE, TILE):
            at = later - first
            to_ref[pl.ds(later, TILE), rows] = value[:, at : at + TILE].T

    for first, at, width in packed_blocks():
        cols = pl.ds(at, width)
        both = mine_ref[:, cols].astype(f32) + other_ref[:, cols].astype(f32)
        store_symmetric(gram_ref, first, (both * scale * scale).astype(bf16))

    def symmetric(to_ref, a_ref, b_ref, finish):
        for first in range(0, WIDE, TILE):
            rows, cols = pl.ds(first, TILE), pl.ds(first, WIDE - first)
            value = finish(rows, cols, mm(a_ref[rows, :], b_ref[:, cols])).astype(bf16)
            store_symmetric(to_ref, first, value)

    def polynomial(g_ref):
        def finish(rows, cols, square):
            return quintic_b * g_ref[rows, cols].astype(f32) + quintic_c * square

        symmetric(poly_ref, g_ref, g_ref, finish)

    def one_side(to_ref, a_ref, b_ref, base_ref):
        def finish(rows, cols, product):
            return quintic_a * base_ref[rows, cols].astype(f32) + product

        symmetric(to_ref, a_ref, b_ref, finish)

    def step(rows):
        return quintic_a * rows.astype(f32) + mm(rows, poly_ref[...])

    polynomial(gram_ref)
    x = step(x).astype(bf16)
    one_side(left_ref, poly_ref, gram_ref, gram_ref)
    one_side(next_ref, left_ref, poly_ref, left_ref)
    polynomial(next_ref)
    x = step(x).astype(bf16)

    def last_gram(rows):
        rows = step(rows).astype(bf16)
        return step(mm(rows, next_ref[...]).astype(bf16))

    once = last_gram(x)
    twice = last_gram(once.astype(bf16))
    x = (quintic_a * x.astype(f32) + (quintic_b * once + quintic_c * twice)).astype(bf16)
    out_ref[...] = (step_scale * x.astype(f32)).astype(bf16)[:2, :FE]


def shape(dims, dtype):
    return jax.ShapeDtypeStruct(dims, dtype)


def exchange(blocks, axes):
    return lax.all_to_all(blocks, axes, 0, 0, tiled=True)


def per_device(activations, cotangent, momentum):
    momentum = momentum[0]
    left = kernel_call(order_kernel, shape((SHARE, 512), bf16), 1, cost=COST)(activations)
    partial = kernel_call(gradient_kernel, shape((SHARE, WIDE), bf16), 2)(left, cotangent.T)
    near = exchange(partial.reshape(16, BLOCK, WIDE), NEAR)
    exact, share = kernel_call(
        share_kernel, (shape((BLOCK, WIDE), f32), shape((8, BLOCK, WIDE), bf16)), 2
    )(near, momentum)
    far = exchange(share, FAR)
    rows, own = kernel_call(
        direction_kernel, (shape((4, BLOCK, WIDE), bf16), shape((16, WIDE), f32)), 2
    )(far, exact)
    rows = exchange(rows, OWNERS).reshape(ROWS, WIDE)
    rows = exchange(kernel_call(pack_kernel, shape((16, PACKED, 128), bf16), 1)(rows), NEAR)
    mine = kernel_call(
        gram_kernel, shape((TILE, 1536), bf16), 1, [pltpu.VMEM((1024, WIDE), bf16)]
    )(rows)
    other = lax.ppermute(mine, "core", [(0, 1), (1, 0)])
    gradient = (own[:2, :FE] - (0.95 * 0.95) * momentum) / 1.95
    momentum_new = 0.95 * momentum + gradient
    update = kernel_call(
        newton_schulz_kernel, shape((2, FE), bf16), 3, [pltpu.VMEM((WIDE, WIDE), bf16)] * 4, mib=48
    )(mine, other, own)
    return (update[None], momentum_new[None])


def solution(mesh):
    fine = Mesh(mesh.devices.reshape(SIZES), AXES)
    tokens, owners = ("x", "ylo", "zhi", "zlo"), ("yhi", "core")
    in_specs = (P(tokens, owners), P(tokens, None), P(owners, tokens, None))
    out_specs = (P(owners, tokens, None), P(owners, tokens, None))
    return jax.shard_map(
        per_device, mesh=fine, in_specs=in_specs, out_specs=out_specs, check_vma=False
    )
```

```python
import jax
import jax.numpy as jnp
from jax import lax
from jax.experimental import pallas as pl
from jax.experimental.pallas import tpu as pltpu
from jax.sharding import Mesh, PartitionSpec as P

DM = 2048
FE = 704
ITERS = 3
WIDE = 768
SHARE = 256
TILE = 256
LINES = 88
TAIL = 640
BLOCK = 16

quintic_a = 3.4445
quintic_b = -4.775
quintic_c = 2.0315
step_scale = 0.2 * max(DM, FE) ** 0.5

AXES = ("x", "ylo", "zhi", "zlo", "yhi", "core")
SIZES = (4, 2, 8, 2, 4, 2)
NEAR = ("x", "ylo", "zlo")
FAR = "zhi"
OWNERS = "yhi"

f32 = jnp.float32
COST = pl.CostEstimate(flops=4_000_000_000, bytes_accessed=1_000_000, transcendentals=0)
bf16 = jnp.bfloat16


def mm(a, b):
    return jnp.dot(a, b, preferred_element_type=f32)


def mm_nt(a, b):
    return lax.dot_general(a, b, (((1,), (1,)), ((), ())), preferred_element_type=f32)


def kernel_call(kernel, out_shape, n_in, scratch=(), mib=32, cost=None):
    return pl.pallas_call(
        kernel,
        out_shape=out_shape,
        in_specs=[pl.BlockSpec(memory_space=pltpu.VMEM)] * n_in,
        out_specs=jax.tree.map(lambda _: pl.BlockSpec(memory_space=pltpu.VMEM), out_shape),
        scratch_shapes=list(scratch),
        cost_estimate=cost,
        compiler_params=pltpu.CompilerParams(vmem_limit_bytes=mib * 1024 * 1024),
    )


def order_kernel(act_ref, out_ref):
    to = lax.broadcasted_iota(jnp.int32, (SHARE, SHARE), 0)
    source = lax.broadcasted_iota(jnp.int32, (SHARE, SHARE), 1)
    wanted = (to & ~31) + ((to & 15) >> 1) * 4 + ((to & 31) >> 4) * 2 + (to & 1)
    order = jnp.where(wanted == source, 1.0, 0.0).astype(bf16)
    out_ref[...] = mm_nt(order, act_ref[...]).astype(bf16)


def lanes(rows):
    return lax.broadcasted_iota(jnp.int32, (rows, 128), 1)


def pack(block):
    tail = block[:, TAIL:]
    last = jnp.where(lanes(8) < 64, tail[:8], pltpu.roll(tail[8:], 64, 1))
    return jnp.concatenate([block[:, at : at + 128] for at in range(0, TAIL, 128)] + [last], axis=0)


def unpack_tail(last):
    upper = jnp.where(lanes(8) < 64, last, 0.0)
    lower = jnp.where(lanes(8) < 64, pltpu.roll(last, 64, 1), 0.0)
    return jnp.concatenate([upper, lower], axis=0)


def unpack(lines):
    tiles = [lines[at // 8 : at // 8 + BLOCK] for at in range(0, TAIL, 128)]
    return jnp.concatenate(tiles + [unpack_tail(lines[LINES - 8 :])], axis=1)


def gradient_kernel(left_ref, cot_ref, out_ref, wide_ref):
    wide_ref[:, :FE] = mm_nt(left_ref[...], cot_ref[...])
    wide_ref[:, FE:] = jnp.zeros((SHARE, WIDE - FE), f32)
    for m in range(SHARE // BLOCK):
        out_ref[m] = pack(wide_ref[m * BLOCK : (m + 1) * BLOCK, :]).astype(bf16)


def own_rows_mask():
    row = lax.broadcasted_iota(jnp.int32, (BLOCK, WIDE), 0)
    return (row >> 1) == lax.axis_index(FAR)


def place_rows(mom_ref):
    row = lax.broadcasted_iota(jnp.int32, (BLOCK, FE), 0)
    first = jnp.broadcast_to(mom_ref[0:1, :], (BLOCK, FE))
    second = jnp.broadcast_to(mom_ref[1:2, :], (BLOCK, FE))
    rows = jnp.where((row & 1) == 0, first, second)
    return jnp.concatenate([rows, jnp.zeros((BLOCK, WIDE - FE), f32)], axis=1)


def share_kernel(near_ref, mom_ref, exact_ref, out_ref):
    partial = jnp.sum(near_ref[...].astype(f32), axis=0)
    own = pack(jnp.where(own_rows_mask(), place_rows(mom_ref), 0.0))
    share = 1.95 * partial + (0.95 * 0.95) * own
    exact_ref[...] = share
    out_ref[...] = jnp.broadcast_to(share.astype(bf16)[None], out_ref.shape)


def direction_kernel(far_ref, exact_ref, rows_ref, own_ref):
    total = jnp.sum(far_ref[...].astype(f32), axis=0)
    rows_ref[...] = jnp.broadcast_to(total.astype(bf16)[None], rows_ref.shape)
    exact = exact_ref[...]
    better = unpack(total + (exact - exact.astype(bf16).astype(f32)))
    mine = jnp.where(own_rows_mask(), better, 0.0)
    odd = (lax.broadcasted_iota(jnp.int32, (BLOCK, WIDE), 0) & 1) == 1
    own_ref[...] = jnp.zeros_like(own_ref)
    own_ref[0:1, :] = jnp.sum(jnp.where(odd, 0.0, mine), axis=0, keepdims=True)
    own_ref[1:2, :] = jnp.sum(jnp.where(odd, mine, 0.0), axis=0, keepdims=True)


def packed_blocks():
    at = 0
    for first in range(0, WIDE, TILE):
        yield first, at, WIDE - first
        at += WIDE - first


def gram_kernel(packed_ref, out_ref, rows_ref):
    for m in range(1024 // BLOCK):
        rows = pl.ds(m * BLOCK, BLOCK)
        for at in range(0, TAIL, 128):
            rows_ref[rows, at : at + 128] = packed_ref[m, at // 8 : at // 8 + BLOCK, :]
        last = packed_ref[m].astype(f32)[LINES - 8 :]
        rows_ref[rows, TAIL:] = unpack_tail(last).astype(bf16)
    for first, at, width in packed_blocks():
        out_ref[:, at : at + width] = lax.dot_general(
            rows_ref[:, first : first + TILE],
            rows_ref[:, first:],
            (((0,), (0,)), ((), ())),
            preferred_element_type=f32,
        ).astype(bf16)


def newton_schulz_kernel(
    mine_ref, other_ref, rows_ref, out_ref, gram_ref, poly_ref, left_ref, next_ref
):
    total = jnp.zeros((128, 128), f32)
    for _, at, _ in packed_blocks():
        for half in range(0, TILE, 128):
            rows, cols = pl.ds(half, 128), pl.ds(at + half, 128)
            total += mine_ref[rows, cols].astype(f32) + other_ref[rows, cols].astype(f32)
    eye = lax.broadcasted_iota(jnp.int32, (128, 128), 0) == lax.broadcasted_iota(
        jnp.int32, (128, 128), 1
    )
    square_sum = jnp.sum(jnp.where(eye, total, 0.0), keepdims=True)
    scale = 1.0 / (jnp.sqrt(square_sum) + 1e-07)
    x = (rows_ref[...] * scale).astype(bf16)

    def store_symmetric(to_ref, first, value):
        rows = pl.ds(first, TILE)
        to_ref[rows, pl.ds(first, WIDE - first)] = value
        for later in range(first + TILE, WIDE, TILE):
            at = later - first
            to_ref[pl.ds(later, TILE), rows] = value[:, at : at + TILE].T

    for first, at, width in packed_blocks():
        cols = pl.ds(at, width)
        both = mine_ref[:, cols].astype(f32) + other_ref[:, cols].astype(f32)
        store_symmetric(gram_ref, first, (both * scale * scale).astype(bf16))

    def symmetric(to_ref, a_ref, b_ref, finish):
        for first in range(0, WIDE, TILE):
            rows, cols = pl.ds(first, TILE), pl.ds(first, WIDE - first)
            value = finish(rows, cols, mm(a_ref[rows, :], b_ref[:, cols])).astype(bf16)
            store_symmetric(to_ref, first, value)

    def polynomial(g_ref):
        def finish(rows, cols, square):
            return quintic_b * g_ref[rows, cols].astype(f32) + quintic_c * square

        symmetric(poly_ref, g_ref, g_ref, finish)

    def one_side(to_ref, a_ref, b_ref, base_ref):
        def finish(rows, cols, product):
            return quintic_a * base_ref[rows, cols].astype(f32) + product

        symmetric(to_ref, a_ref, b_ref, finish)

    def step(rows):
        return quintic_a * rows.astype(f32) + mm(rows, poly_ref[...])

    polynomial(gram_ref)
    x = step(x).astype(bf16)
    one_side(left_ref, poly_ref, gram_ref, gram_ref)
    one_side(next_ref, left_ref, poly_ref, left_ref)
    polynomial(next_ref)
    x = step(x).astype(bf16)

    def last_gram(rows):
        rows = step(rows).astype(bf16)
        return step(mm(rows, next_ref[...]).astype(bf16))

    once = last_gram(x)
    twice = last_gram(once.astype(bf16))
    x = (quintic_a * x.astype(f32) + (quintic_b * once + quintic_c * twice)).astype(bf16)
    out_ref[...] = (step_scale * x.astype(f32)).astype(bf16)[:2, :FE]


def shape(dims, dtype):
    return jax.ShapeDtypeStruct(dims, dtype)


def exchange(blocks, axes):
    return lax.all_to_all(blocks, axes, 0, 0, tiled=True)


def per_device(activations, cotangent, momentum):
    momentum = momentum[0]
    left = kernel_call(order_kernel, shape((SHARE, 512), bf16), 1, cost=COST)(activations)
    partial = kernel_call(
        gradient_kernel, shape((16, LINES, 128), bf16), 2, [pltpu.VMEM((SHARE, WIDE), f32)]
    )(left, cotangent.T)
    near = exchange(partial, NEAR)
    exact, share = kernel_call(
        share_kernel, (shape((LINES, 128), f32), shape((8, LINES, 128), bf16)), 2
    )(near, momentum)
    far = exchange(share, FAR)
    rows, own = kernel_call(
        direction_kernel, (shape((4, LINES, 128), bf16), shape((16, WIDE), f32)), 2
    )(far, exact)
    rows = exchange(rows, OWNERS)
    rows = exchange(jnp.broadcast_to(rows[None], (16, 4, LINES, 128)), NEAR)
    mine = kernel_call(
        gram_kernel, shape((TILE, 1536), bf16), 1, [pltpu.VMEM((1024, WIDE), bf16)]
    )(rows.reshape(64, LINES, 128))
    other = lax.ppermute(mine, "core", [(0, 1), (1, 0)])
    gradient = (own[:2, :FE] - (0.95 * 0.95) * momentum) / 1.95
    momentum_new = 0.95 * momentum + gradient
    update = kernel_call(
        newton_schulz_kernel, shape((2, FE), bf16), 3, [pltpu.VMEM((WIDE, WIDE), bf16)] * 4, mib=48
    )(mine, other, own)
    return (update[None], momentum_new[None])


def solution(mesh):
    fine = Mesh(mesh.devices.reshape(SIZES), AXES)
    tokens, owners = ("x", "ylo", "zhi", "zlo"), ("yhi", "core")
    in_specs = (P(tokens, owners), P(tokens, None), P(owners, tokens, None))
    out_specs = (P(owners, tokens, None), P(owners, tokens, None))
    return jax.shard_map(
        per_device, mesh=fine, in_specs=in_specs, out_specs=out_specs, check_vma=False
    )
```

```python
import jax
import jax.numpy as jnp
from jax import lax
from jax.experimental import pallas as pl
from jax.experimental.pallas import tpu as pltpu
from jax.sharding import Mesh, PartitionSpec as P

DM = 2048
FE = 704
ITERS = 3
WIDE = 768
SHARE = 256
TILE = 256
LINES = 88
TAIL = 640
BLOCK = 16

quintic_a = 3.4445
quintic_b = -4.775
quintic_c = 2.0315
step_scale = 0.2 * max(DM, FE) ** 0.5

AXES = ("x", "ylo", "zhi", "zlo", "yhi", "core")
SIZES = (4, 2, 8, 2, 4, 2)
NEAR = ("x", "ylo", "zlo")
FAR = "zhi"
OWNERS = "yhi"
FAR_ORDER = [[0, 4, 2, 6, 1, 5, 3, 7]]

f32 = jnp.float32
COST = pl.CostEstimate(flops=4_000_000_000, bytes_accessed=1_000_000, transcendentals=0)
bf16 = jnp.bfloat16


def mm(a, b):
    return jnp.dot(a, b, preferred_element_type=f32)


def mm_nt(a, b):
    return lax.dot_general(a, b, (((1,), (1,)), ((), ())), preferred_element_type=f32)


def kernel_call(kernel, out_shape, n_in, scratch=(), mib=32, cost=None):
    return pl.pallas_call(
        kernel,
        out_shape=out_shape,
        in_specs=[pl.BlockSpec(memory_space=pltpu.VMEM)] * n_in,
        out_specs=jax.tree.map(lambda _: pl.BlockSpec(memory_space=pltpu.VMEM), out_shape),
        scratch_shapes=list(scratch),
        cost_estimate=cost,
        compiler_params=pltpu.CompilerParams(vmem_limit_bytes=mib * 1024 * 1024),
    )


def order_kernel(act_ref, out_ref):
    to = lax.broadcasted_iota(jnp.int32, (SHARE, SHARE), 0)
    source = lax.broadcasted_iota(jnp.int32, (SHARE, SHARE), 1)
    wanted = (to & ~31) + ((to & 15) >> 1) * 4 + ((to & 31) >> 4) * 2 + (to & 1)
    order = jnp.where(wanted == source, 1.0, 0.0).astype(bf16)
    out_ref[...] = mm_nt(order, act_ref[...]).astype(bf16)


def lanes(rows):
    return lax.broadcasted_iota(jnp.int32, (rows, 128), 1)


def pack(block):
    tail = block[:, TAIL:]
    last = jnp.where(lanes(8) < 64, tail[:8], pltpu.roll(tail[8:], 64, 1))
    return jnp.concatenate([block[:, at : at + 128] for at in range(0, TAIL, 128)] + [last], axis=0)


def unpack_tail(last):
    upper = jnp.where(lanes(8) < 64, last, 0.0)
    lower = jnp.where(lanes(8) < 64, pltpu.roll(last, 64, 1), 0.0)
    return jnp.concatenate([upper, lower], axis=0)


def unpack(lines):
    tiles = [lines[at // 8 : at // 8 + BLOCK] for at in range(0, TAIL, 128)]
    return jnp.concatenate(tiles + [unpack_tail(lines[LINES - 8 :])], axis=1)


def gradient_kernel(left_ref, cot_ref, out_ref, wide_ref):
    wide_ref[:, :FE] = mm_nt(left_ref[...], cot_ref[...])
    wide_ref[:, FE:] = jnp.zeros((SHARE, WIDE - FE), f32)
    for m in range(SHARE // BLOCK):
        out_ref[m] = pack(wide_ref[m * BLOCK : (m + 1) * BLOCK, :]).astype(bf16)


def own_rows_mask():
    row = lax.broadcasted_iota(jnp.int32, (BLOCK, WIDE), 0)
    return (row >> 1) == lax.axis_index(FAR)


def place_rows(mom_ref):
    row = lax.broadcasted_iota(jnp.int32, (BLOCK, FE), 0)
    first = jnp.broadcast_to(mom_ref[0:1, :], (BLOCK, FE))
    second = jnp.broadcast_to(mom_ref[1:2, :], (BLOCK, FE))
    rows = jnp.where((row & 1) == 0, first, second)
    return jnp.concatenate([rows, jnp.zeros((BLOCK, WIDE - FE), f32)], axis=1)


def share_kernel(near_ref, mom_ref, exact_ref, out_ref):
    partial = jnp.sum(near_ref[...].astype(f32), axis=0)
    own = pack(jnp.where(own_rows_mask(), place_rows(mom_ref), 0.0))
    share = 1.95 * partial + (0.95 * 0.95) * own
    exact_ref[...] = share
    out_ref[...] = jnp.broadcast_to(share.astype(bf16)[None], out_ref.shape)


def direction_kernel(far_ref, exact_ref, rows_ref, own_ref):
    total = jnp.sum(far_ref[...].astype(f32), axis=0)
    rows_ref[...] = jnp.broadcast_to(total.astype(bf16)[None], rows_ref.shape)
    exact = exact_ref[...]
    better = unpack(total + (exact - exact.astype(bf16).astype(f32)))
    mine = jnp.where(own_rows_mask(), better, 0.0)
    odd = (lax.broadcasted_iota(jnp.int32, (BLOCK, WIDE), 0) & 1) == 1
    first = jnp.sum(jnp.where(odd, 0.0, mine), axis=0, keepdims=True)
    second = jnp.sum(jnp.where(odd, mine, 0.0), axis=0, keepdims=True)
    row = lax.broadcasted_iota(jnp.int32, (16, WIDE), 0)
    own_ref[...] = jnp.where(row < 6, jnp.where((row & 1) == 0, first, second), 0.0)


def packed_blocks():
    at = 0
    for first in range(0, WIDE, TILE):
        yield first, at, WIDE - first
        at += WIDE - first


def gram_kernel(packed_ref, out_ref, rows_ref):
    for m in range(1024 // BLOCK):
        rows = pl.ds(m * BLOCK, BLOCK)
        for at in range(0, TAIL, 128):
            rows_ref[rows, at : at + 128] = packed_ref[m, at // 8 : at // 8 + BLOCK, :]
        last = packed_ref[m].astype(f32)[LINES - 8 :]
        rows_ref[rows, TAIL:] = unpack_tail(last).astype(bf16)
    for first, at, width in packed_blocks():
        out_ref[:, at : at + width] = lax.dot_general(
            rows_ref[:, first : first + TILE],
            rows_ref[:, first:],
            (((0,), (0,)), ((), ())),
            preferred_element_type=f32,
        ).astype(bf16)


def newton_schulz_kernel(
    mine_ref, other_ref, rows_ref, out_ref, gram_ref, poly_ref, left_ref, next_ref
):
    total = jnp.zeros((128, 128), f32)
    for _, at, _ in packed_blocks():
        for half in range(0, TILE, 128):
            rows, cols = pl.ds(half, 128), pl.ds(at + half, 128)
            total += mine_ref[rows, cols].astype(f32) + other_ref[rows, cols].astype(f32)
    eye = lax.broadcasted_iota(jnp.int32, (128, 128), 0) == lax.broadcasted_iota(
        jnp.int32, (128, 128), 1
    )
    square_sum = jnp.sum(jnp.where(eye, total, 0.0), keepdims=True)
    scale = 1.0 / (jnp.sqrt(square_sum) + 1e-07)
    x = (rows_ref[...] * scale).astype(bf16)

    def store_symmetric(to_ref, first, value):
        rows = pl.ds(first, TILE)
        to_ref[rows, pl.ds(first, WIDE - first)] = value
        for later in range(first + TILE, WIDE, TILE):
            at = later - first
            to_ref[pl.ds(later, TILE), rows] = value[:, at : at + TILE].T

    for first, at, width in packed_blocks():
        cols = pl.ds(at, width)
        both = mine_ref[:, cols].astype(f32) + other_ref[:, cols].astype(f32)
        store_symmetric(gram_ref, first, (both * scale * scale).astype(bf16))

    def symmetric(to_ref, a_ref, b_ref, finish):
        for first in range(0, WIDE, TILE):
            rows, cols = pl.ds(first, TILE), pl.ds(first, WIDE - first)
            value = finish(rows, cols, mm(a_ref[rows, :], b_ref[:, cols])).astype(bf16)
            store_symmetric(to_ref, first, value)

    def polynomial(g_ref):
        def finish(rows, cols, square):
            return quintic_b * g_ref[rows, cols].astype(f32) + quintic_c * square

        symmetric(poly_ref, g_ref, g_ref, finish)

    def one_side(to_ref, a_ref, b_ref, base_ref):
        def finish(rows, cols, product):
            return quintic_a * base_ref[rows, cols].astype(f32) + product

        symmetric(to_ref, a_ref, b_ref, finish)

    def step(rows):
        return quintic_a * rows.astype(f32) + mm(rows, poly_ref[...])

    polynomial(gram_ref)
    x = step(x).astype(bf16)
    one_side(left_ref, poly_ref, gram_ref, gram_ref)
    one_side(next_ref, left_ref, poly_ref, left_ref)
    group = lax.broadcasted_iota(jnp.int32, (16, WIDE), 0) >> 1
    stack = jnp.where(group == 0, x.astype(f32), mm(x, next_ref[...]))
    stack = jnp.where(group == 2, mm(stack.astype(bf16), next_ref[...]), stack)
    polynomial(next_ref)
    powers = []
    for _ in range(5):
        stack = step(stack.astype(bf16))
        powers.append(stack)
    x = powers[0][:2].astype(bf16).astype(f32)
    once, twice = powers[2][2:4], powers[4][4:6]
    x = (quintic_a * x + (quintic_b * once + quintic_c * twice)).astype(bf16)
    out_ref[...] = (step_scale * x.astype(f32)).astype(bf16)[:, :FE]


def shape(dims, dtype):
    return jax.ShapeDtypeStruct(dims, dtype)


def exchange(blocks, axes):
    return lax.all_to_all(blocks, axes, 0, 0, tiled=True)


def per_device(activations, cotangent, momentum):
    momentum = momentum[0]
    left = kernel_call(order_kernel, shape((SHARE, 512), bf16), 1, cost=COST)(activations)
    partial = kernel_call(
        gradient_kernel, shape((16, LINES, 128), bf16), 2, [pltpu.VMEM((SHARE, WIDE), f32)]
    )(left, cotangent.T)
    near = exchange(partial, NEAR)
    exact, share = kernel_call(
        share_kernel, (shape((LINES, 128), f32), shape((8, LINES, 128), bf16)), 2
    )(near, momentum)
    far = lax.all_to_all(share, FAR, 0, 0, axis_index_groups=FAR_ORDER, tiled=True)
    rows, own = kernel_call(
        direction_kernel, (shape((4, LINES, 128), bf16), shape((16, WIDE), f32)), 2
    )(far, exact)
    rows = exchange(rows, OWNERS)
    rows = exchange(jnp.broadcast_to(rows[None], (16, 4, LINES, 128)), NEAR)
    mine = kernel_call(
        gram_kernel, shape((TILE, 1536), bf16), 1, [pltpu.VMEM((1024, WIDE), bf16)]
    )(rows.reshape(64, LINES, 128))
    other = lax.ppermute(mine, "core", [(0, 1), (1, 0)])
    gradient = (own[:2, :FE] - (0.95 * 0.95) * momentum) / 1.95
    momentum_new = 0.95 * momentum + gradient
    update = kernel_call(
        newton_schulz_kernel, shape((2, FE), bf16), 3, [pltpu.VMEM((WIDE, WIDE), bf16)] * 4, mib=48
    )(mine, other, own)
    return (update[None], momentum_new[None])


def solution(mesh):
    fine = Mesh(mesh.devices.reshape(SIZES), AXES)
    tokens, owners = ("x", "ylo", "zhi", "zlo"), ("yhi", "core")
    in_specs = (P(tokens, owners), P(tokens, None), P(owners, tokens, None))
    out_specs = (P(owners, tokens, None), P(owners, tokens, None))
    return jax.shard_map(
        per_device, mesh=fine, in_specs=in_specs, out_specs=out_specs, check_vma=False
    )
```

```python
import jax
import jax.numpy as jnp
from jax import lax
from jax.experimental import pallas as pl
from jax.experimental.pallas import tpu as pltpu
from jax.sharding import Mesh, PartitionSpec as P

DM = 2048
FE = 704
ITERS = 3
WIDE = 768
SHARE = 256
TILE = 256
LINES = 88
TAIL = 640
BLOCK = 16

quintic_a = 3.4445
quintic_b = -4.775
quintic_c = 2.0315
step_scale = 0.2 * max(DM, FE) ** 0.5

AXES = ("x", "ylo", "zhi", "zlo", "yhi", "core")
SIZES = (4, 2, 8, 2, 4, 2)
NEAR = ("x", "ylo", "zlo")
FAR = "zhi"
FAR_ORDER = [[0, 4, 2, 6, 1, 5, 3, 7]]
OWNERS = ('ylo', 'yhi')
LAST = ('x', 'zlo')

f32 = jnp.float32
COST = pl.CostEstimate(flops=4_000_000_000, bytes_accessed=1_000_000, transcendentals=0)
bf16 = jnp.bfloat16


def mm(a, b):
    return jnp.dot(a, b, preferred_element_type=f32)


def mm_nt(a, b):
    return lax.dot_general(a, b, (((1,), (1,)), ((), ())), preferred_element_type=f32)


def kernel_call(kernel, out_shape, n_in, scratch=(), mib=32, cost=None):
    return pl.pallas_call(
        kernel,
        out_shape=out_shape,
        in_specs=[pl.BlockSpec(memory_space=pltpu.VMEM)] * n_in,
        out_specs=jax.tree.map(lambda _: pl.BlockSpec(memory_space=pltpu.VMEM), out_shape),
        scratch_shapes=list(scratch),
        cost_estimate=cost,
        compiler_params=pltpu.CompilerParams(vmem_limit_bytes=mib * 1024 * 1024),
    )


def order_kernel(act_ref, out_ref):
    to = lax.broadcasted_iota(jnp.int32, (SHARE, SHARE), 0)
    source = lax.broadcasted_iota(jnp.int32, (SHARE, SHARE), 1)
    wanted = (to & ~31) + ((to & 15) >> 1) * 4 + ((to & 31) >> 4) * 2 + (to & 1)
    order = jnp.where(wanted == source, 1.0, 0.0).astype(bf16)
    out_ref[...] = mm_nt(order, act_ref[...]).astype(bf16)


def lanes(rows):
    return lax.broadcasted_iota(jnp.int32, (rows, 128), 1)


def pack(block):
    tail = block[:, TAIL:]
    last = jnp.where(lanes(8) < 64, tail[:8], pltpu.roll(tail[8:], 64, 1))
    return jnp.concatenate([block[:, at : at + 128] for at in range(0, TAIL, 128)] + [last], axis=0)


def unpack_tail(last):
    upper = jnp.where(lanes(8) < 64, last, 0.0)
    lower = jnp.where(lanes(8) < 64, pltpu.roll(last, 64, 1), 0.0)
    return jnp.concatenate([upper, lower], axis=0)


def unpack(lines):
    tiles = [lines[at // 8 : at // 8 + BLOCK] for at in range(0, TAIL, 128)]
    return jnp.concatenate(tiles + [unpack_tail(lines[LINES - 8 :])], axis=1)


def gradient_kernel(left_ref, cot_ref, out_ref, wide_ref):
    wide_ref[:, :FE] = mm_nt(left_ref[...], cot_ref[...])
    wide_ref[:, FE:] = jnp.zeros((SHARE, WIDE - FE), f32)
    for m in range(SHARE // BLOCK):
        out_ref[m] = pack(wide_ref[m * BLOCK : (m + 1) * BLOCK, :]).astype(bf16)


def own_rows_mask():
    row = lax.broadcasted_iota(jnp.int32, (BLOCK, WIDE), 0)
    return (row >> 1) == lax.axis_index(FAR)


def place_rows(mom_ref):
    row = lax.broadcasted_iota(jnp.int32, (BLOCK, FE), 0)
    first = jnp.broadcast_to(mom_ref[0:1, :], (BLOCK, FE))
    second = jnp.broadcast_to(mom_ref[1:2, :], (BLOCK, FE))
    rows = jnp.where((row & 1) == 0, first, second)
    return jnp.concatenate([rows, jnp.zeros((BLOCK, WIDE - FE), f32)], axis=1)


def share_kernel(near_ref, mom_ref, exact_ref, out_ref):
    partial = jnp.sum(near_ref[...].astype(f32), axis=0)
    own = pack(jnp.where(own_rows_mask(), place_rows(mom_ref), 0.0))
    share = 1.95 * partial + (0.95 * 0.95) * own
    exact_ref[...] = share
    out_ref[...] = jnp.broadcast_to(share.astype(bf16)[None], out_ref.shape)


def direction_kernel(far_ref, exact_ref, rows_ref, own_ref):
    total = jnp.sum(far_ref[...].astype(f32), axis=0)
    rows_ref[...] = jnp.broadcast_to(total.astype(bf16)[None], rows_ref.shape)
    exact = exact_ref[...]
    better = unpack(total + (exact - exact.astype(bf16).astype(f32)))
    mine = jnp.where(own_rows_mask(), better, 0.0)
    odd = (lax.broadcasted_iota(jnp.int32, (BLOCK, WIDE), 0) & 1) == 1
    own_ref[...] = jnp.zeros_like(own_ref)
    own_ref[0:1, :] = jnp.sum(jnp.where(odd, 0.0, mine), axis=0, keepdims=True)
    own_ref[1:2, :] = jnp.sum(jnp.where(odd, mine, 0.0), axis=0, keepdims=True)


def packed_blocks():
    at = 0
    for first in range(0, WIDE, TILE):
        yield first, at, WIDE - first
        at += WIDE - first


def gram_kernel(packed_ref, out_ref, rows_ref):
    for m in range(1024 // BLOCK):
        rows = pl.ds(m * BLOCK, BLOCK)
        for at in range(0, TAIL, 128):
            rows_ref[rows, at : at + 128] = packed_ref[m, at // 8 : at // 8 + BLOCK, :]
        last = packed_ref[m].astype(f32)[LINES - 8 :]
        rows_ref[rows, TAIL:] = unpack_tail(last).astype(bf16)
    for first, at, width in packed_blocks():
        out_ref[:, at : at + width] = lax.dot_general(
            rows_ref[:, first : first + TILE],
            rows_ref[:, first:],
            (((0,), (0,)), ((), ())),
            preferred_element_type=f32,
        ).astype(bf16)


def newton_schulz_kernel(
    mine_ref, other_ref, rows_ref, out_ref, gram_ref, poly_ref, left_ref, next_ref
):
    total = jnp.zeros((128, 128), f32)
    for _, at, _ in packed_blocks():
        for half in range(0, TILE, 128):
            rows, cols = pl.ds(half, 128), pl.ds(at + half, 128)
            total += mine_ref[rows, cols].astype(f32) + other_ref[rows, cols].astype(f32)
    eye = lax.broadcasted_iota(jnp.int32, (128, 128), 0) == lax.broadcasted_iota(
        jnp.int32, (128, 128), 1
    )
    square_sum = jnp.sum(jnp.where(eye, total, 0.0), keepdims=True)
    scale = 1.0 / (jnp.sqrt(square_sum) + 1e-07)
    x = (rows_ref[...] * scale).astype(bf16)

    def store_symmetric(to_ref, first, value):
        rows = pl.ds(first, TILE)
        to_ref[rows, pl.ds(first, WIDE - first)] = value
        for later in range(first + TILE, WIDE, TILE):
            at = later - first
            to_ref[pl.ds(later, TILE), rows] = value[:, at : at + TILE].T

    for first, at, width in packed_blocks():
        cols = pl.ds(at, width)
        both = mine_ref[:, cols].astype(f32) + other_ref[:, cols].astype(f32)
        store_symmetric(gram_ref, first, (both * scale * scale).astype(bf16))

    def symmetric(to_ref, a_ref, b_ref, finish):
        for first in range(0, WIDE, TILE):
            rows, cols = pl.ds(first, TILE), pl.ds(first, WIDE - first)
            value = finish(rows, cols, mm(a_ref[rows, :], b_ref[:, cols])).astype(bf16)
            store_symmetric(to_ref, first, value)

    def polynomial(g_ref):
        def finish(rows, cols, square):
            return quintic_b * g_ref[rows, cols].astype(f32) + quintic_c * square

        symmetric(poly_ref, g_ref, g_ref, finish)

    def one_side(to_ref, a_ref, b_ref, base_ref):
        def finish(rows, cols, product):
            return quintic_a * base_ref[rows, cols].astype(f32) + product

        symmetric(to_ref, a_ref, b_ref, finish)

    def step(rows):
        return quintic_a * rows.astype(f32) + mm(rows, poly_ref[...])

    polynomial(gram_ref)
    x = step(x).astype(bf16)
    one_side(left_ref, poly_ref, gram_ref, gram_ref)
    one_side(next_ref, left_ref, poly_ref, left_ref)
    polynomial(next_ref)
    x = step(x).astype(bf16)

    def last_gram(rows):
        rows = step(rows).astype(bf16)
        return step(mm(rows, next_ref[...]).astype(bf16))

    once = last_gram(x)
    twice = last_gram(once.astype(bf16))
    x = (quintic_a * x.astype(f32) + (quintic_b * once + quintic_c * twice)).astype(bf16)
    out_ref[...] = (step_scale * x.astype(f32)).astype(bf16)[:2, :FE]


def shape(dims, dtype):
    return jax.ShapeDtypeStruct(dims, dtype)


def exchange(blocks, axes):
    return lax.all_to_all(blocks, axes, 0, 0, tiled=True)


def per_device(activations, cotangent, momentum):
    momentum = momentum[0]
    left = kernel_call(order_kernel, shape((SHARE, 512), bf16), 1, cost=COST)(activations)
    partial = kernel_call(
        gradient_kernel, shape((16, LINES, 128), bf16), 2, [pltpu.VMEM((SHARE, WIDE), f32)]
    )(left, cotangent.T)
    near = exchange(partial, NEAR)
    exact, share = kernel_call(
        share_kernel, (shape((LINES, 128), f32), shape((8, LINES, 128), bf16)), 2
    )(near, momentum)
    far = lax.all_to_all(share, FAR, 0, 0, axis_index_groups=FAR_ORDER, tiled=True)
    rows, own = kernel_call(
        direction_kernel, (shape((8, LINES, 128), bf16), shape((16, WIDE), f32)), 2
    )(far, exact)
    rows = exchange(rows, OWNERS)
    rows = exchange(jnp.broadcast_to(rows[None], (8, 8, LINES, 128)), LAST)
    mine = kernel_call(
        gram_kernel, shape((TILE, 1536), bf16), 1, [pltpu.VMEM((1024, WIDE), bf16)]
    )(rows.reshape(64, LINES, 128))
    other = lax.ppermute(mine, "core", [(0, 1), (1, 0)])
    gradient = (own[:2, :FE] - (0.95 * 0.95) * momentum) / 1.95
    momentum_new = 0.95 * momentum + gradient
    update = kernel_call(
        newton_schulz_kernel, shape((2, FE), bf16), 3, [pltpu.VMEM((WIDE, WIDE), bf16)] * 4, mib=48
    )(mine, other, own)
    return (update[None], momentum_new[None])


def solution(mesh):
    fine = Mesh(mesh.devices.reshape(SIZES), AXES)
    tokens, owners = ("x", "ylo", "zhi", "zlo"), ("yhi", "core")
    in_specs = (P(tokens, owners), P(tokens, None), P(owners, tokens, None))
    out_specs = (P(owners, tokens, None), P(owners, tokens, None))
    return jax.shard_map(
        per_device, mesh=fine, in_specs=in_specs, out_specs=out_specs, check_vma=False
    )
```
